32 devices in a mesh: fsdp: 4 (over x, core), ctx: 4 (over z), ch: 2 (over y).
Axes of the slice: x: 2, y: 2, z: 4, core: 2. Of those that a mesh axis runs over, the one named last changes fastest.
Arguments:
- tokens: bfloat16 [4096, 4096], P(('fsdp', 'ctx'), 'ch'), may hold values from -6 to 6
- w_query: bfloat16 [4096, 2048], P(('fsdp', 'ctx'), 'ch'), may hold values from -0.09375 to 0.09375
- w_key: bfloat16 [4096, 2048], P(('fsdp', 'ctx'), 'ch'), may hold values from -0.09375 to 0.09375
- w_value: bfloat16 [4096, 2048], P(('fsdp', 'ctx'), 'ch'), may hold values from -0.09375 to 0.09375
- short_taps: float32 [3, 3, 2048], P(None, None, 'ch'), may hold values from -3 to 3
- long_filter: float32 [4096, 2048], P(('fsdp', 'ctx'), 'ch'), may hold values from -6 to 6
- filter_bias: float32 [2048], P('ch'), may hold values from -4 to 4
Outputs:
- mixed_out: bfloat16 [4096, 2048], P(('fsdp', 'ctx'), 'ch')
The draws below stay inside these ranges and needn't reach their ends.
All inputs are finite; a program needn't handle non-finite values.
Results may differ from the reference program's by a relative error of at most 0.0064.
Values may be sent and summed in bfloat16 or wider, within the bound.
No kernel may reach another device: no remote copies, remote signals or barrier semaphores. Data moves between devices by JAX's collectives and lax.ppermute only.
A program may use at most 128 MiB of HBM per device.

```python
import math
import jax
import jax.numpy as jnp

D = 4096
C = 2048
SEQ = 4096


def draw_long_filter(key, part):
    key = jax.random.fold_in(key, 7)
    rate_key, body_key = jax.random.split(key, 2)
    lowest = math.log(40.0)
    highest = math.log(40.0 * SEQ)
    reach = jnp.exp(jax.random.uniform(rate_key, (C,), jnp.float32, lowest, highest))
    times = jnp.arange(SEQ, dtype=jnp.float32)[:, None]
    envelope = jnp.exp(-times / reach[None, :])
    energy = -jnp.expm1(-2.0 * SEQ / reach) / -jnp.expm1(-2.0 / reach)
    rough = jnp.clip(jax.random.normal(body_key, (SEQ, C), jnp.float32), -6.0, 6.0)
    return rough * envelope / jnp.sqrt(energy)[None, :]


def levels(key, dims, cuts, low, largest):
    loudness, own = 1.0, jax.random.fold_in(key, 6)
    for axis_at, shards_of in cuts:
        draws = jnp.exp(jax.random.uniform(jax.random.fold_in(own, axis_at), (shards_of,), jnp.float32, low / len(cuts), largest / len(cuts)))
        loudness = loudness * jnp.repeat(draws, dims[axis_at] // shards_of).reshape([-1 if axis == axis_at else 1 for axis in range(len(dims))])
    return loudness


def bell_draw(key, dims, spread, most, pieces=(), kind=jnp.bfloat16):
    gain = levels(key, dims, pieces, -0.22, 0.18) if pieces else 1.0
    array = jax.random.normal(key, dims, jnp.float32) * spread * gain
    return jnp.minimum(jnp.maximum(array, -most), most).astype(kind)


def setup_inputs(seed: int = 0) -> dict:
    seeds = jax.random.split(jax.random.key(seed), 8)
    return {
        "tokens": bell_draw(seeds[0], (SEQ, D), 1.0, 6.0, ((0, 16), (1, 2))),
        "w_query": bell_draw(seeds[1], (D, C), D ** -0.5, 0.09375, ((0, 16), (1, 2))),
        "w_key": bell_draw(seeds[2], (D, C), D ** -0.5, 0.09375, ((0, 16), (1, 2))),
        "w_value": bell_draw(seeds[3], (D, C), D ** -0.5, 0.09375, ((0, 16), (1, 2))),
        "short_taps": bell_draw(seeds[4], (3, 3, C), 0.6, 3.0, ((2, 2),), jnp.float32),
        "long_filter": draw_long_filter(jax.random.fold_in(seeds[7], 71), 0),
        "filter_bias": bell_draw(seeds[6], (C,), 1.0, 4.0, ((0, 2),), jnp.float32),
    }


def short_conv(stream, taps):
    values = stream.astype(jnp.float32)
    padded = jnp.pad(values, ((2, 0), (0, 0)))
    return taps[0] * values + taps[1] * padded[1:1 + SEQ] + taps[2] * padded[0:SEQ]


def reference(tokens, w_query, w_key, w_value, short_taps, long_filter, filter_bias):
    query = jnp.dot(tokens, w_query, preferred_element_type=jnp.float32).astype(jnp.bfloat16)
    key_proj = jnp.dot(tokens, w_key, preferred_element_type=jnp.float32).astype(jnp.bfloat16)
    value = jnp.dot(tokens, w_value, preferred_element_type=jnp.float32).astype(jnp.bfloat16)
    query_conv = short_conv(query, short_taps[0])
    key_conv = short_conv(key_proj, short_taps[1])
    value_conv = short_conv(value, short_taps[2])
    gated = key_conv * value_conv
    length = 2 * SEQ
    spectrum = jnp.fft.rfft(gated, n=length, axis=0) * jnp.fft.rfft(long_filter, n=length, axis=0)
    conv = jnp.fft.irfft(spectrum, n=length, axis=0)[:SEQ]
    return (query_conv * (conv + filter_bias[None, :] * gated)).astype(jnp.bfloat16)
```

```python
import functools
import math

import jax
import jax.numpy as jnp
from jax import lax
from jax.experimental import pallas as pl
from jax.experimental.pallas import tpu as pltpu
from jax.sharding import Mesh, PartitionSpec as P

LANES = 128
STEP = 64
WIDE = 512
HALO = 16
ROWS = ("fr", "fc", "cr", "cc")
F32 = jnp.float32
BF16 = jnp.bfloat16


def swap(x, axis, bits):
    size = lax.axis_size(axis)
    return lax.ppermute(x, axis, [(i, i ^ bits) for i in range(size)])


def put(buffer, piece, starts):
    return lax.dynamic_update_slice(buffer, piece, [jnp.int32(s) for s in starts])


def toeplitz_body(h_ref, t_ref):
    channels, chunks, _ = h_ref.shape
    sub = lax.broadcasted_iota(jnp.int32, (STEP, LANES), 0)
    lane = lax.broadcasted_iota(jnp.int32, (STEP, LANES), 1)
    keep = lane >= sub
    for c in range(channels):
        last = jnp.zeros((STEP, LANES), F32)
        for j in range(chunks):
            row = jnp.broadcast_to(h_ref[c, j : j + 1, :].astype(F32), (STEP, LANES))
            now = pltpu.roll(row, 0, 1, stride=1, stride_axis=0)
            block, part = divmod(j, WIDE // LANES)
            t_ref[c, block * STEP : (block + 1) * STEP, part * LANES : (part + 1) * LANES] = jnp.where(
                keep, now, last
            ).astype(BF16)
            last = now


def toeplitz(filters):
    channels, chunks, _ = filters.shape
    depth = chunks * LANES // WIDE * STEP
    group = min(4, channels)
    return pl.pallas_call(
        toeplitz_body,
        grid=(channels // group,),
        in_specs=[pl.BlockSpec((group, chunks, LANES), lambda i: (i, 0, 0))],
        out_specs=pl.BlockSpec((group, depth, WIDE), lambda i: (i, 0, 0)),
        out_shape=jax.ShapeDtypeStruct((channels, depth, WIDE), BF16),
        compiler_params=pltpu.CompilerParams(vmem_limit_bytes=60 << 20),
        cost_estimate=pl.CostEstimate(
            flops=channels * depth * WIDE * 4, bytes_accessed=channels * depth * WIDE * 2, transcendentals=0
        ),
        name="toeplitz",
    )(filters)


def down(x, rows):
    at = lax.broadcasted_iota(jnp.int32, x.shape, 0)
    return jnp.where(at >= rows, pltpu.roll(x, rows, 0), 0.0)


def conv_body(keys, sizes, place, *refs):
    pieces = dict(zip(keys, refs))
    t_ref, bias_ref, o_ref, held, folded = refs[len(keys) :]
    fr_n, fc_n, cr_n, cc_n = sizes
    channels = bias_ref.shape[0]
    rows = folded.shape[0] // channels
    lag = WIDE // STEP
    low = lax.broadcasted_iota(jnp.int32, (channels, LANES), 1) < STEP
    low_rows = lax.broadcasted_iota(jnp.int32, (rows, LANES), 1) < STEP
    bias = bias_ref[...]
    held[0 : lag * channels, :] = jnp.zeros((lag * channels, LANES), F32)

    def spans():
        for (d, a), ref in pieces.items():
            for f in range(fc_n):
                for c in range(cc_n):
                    span = (((place[0] ^ d) * fc_n + f) * cr_n + (place[2] ^ a)) * cc_n + c
                    yield span, ref[f * cc_n + c].astype(F32)

    def lines(row):
        return pl.ds(pl.multiple_of(row * channels, channels), channels)

    for span, gated in spans():
        for k in range(4):
            half = gated[:, (k // 2) * LANES : (k // 2 + 1) * LANES]
            other = pltpu.roll(half, STEP, 1)
            twice = jnp.where(low, half, other) if k % 2 == 0 else jnp.where(low, other, half)
            held[lines(lag + 4 * span + k), :] = twice
    for c in range(channels):
        line = held[pl.ds(c, rows + lag, stride=channels), :]
        pair = jnp.where(low_rows, line[lag:], line[:rows]).astype(BF16)
        parts = [pair]
        for q in range(1, rows // (2 * lag)):
            shift = 2 * lag * q
            parts.append(jnp.concatenate([jnp.zeros((shift, LANES), BF16), pair[: rows - shift]], axis=0))
        left = jnp.concatenate(parts, axis=1)
        wide = jnp.dot(left, t_ref[c], preferred_element_type=F32)
        half_wide = WIDE // 2
        wide = wide[:, :half_wide] + down(wide[:, half_wide:], half_wide // STEP)
        wide = wide[:, :LANES] + down(wide[:, LANES:], 2)
        folded[pl.ds(c, rows, stride=channels), :] = wide + down(pltpu.roll(wide, STEP, 1), 1)
    for span, gated in spans():
        parts = [folded[lines(4 * span + k), :] for k in range(4)]
        for k in range(2):
            conv = jnp.where(low, parts[2 * k], pltpu.roll(parts[2 * k + 1], STEP, 1))
            cut = slice(k * LANES, (k + 1) * LANES)
            o_ref[span, :, cut] = (conv + bias * gated[:, cut]).astype(BF16)


def long_conv(place, pieces, blocks, bias, sizes):
    few, depth = blocks.shape[:2]
    count = math.prod(sizes)
    some = next(iter(pieces.values()))
    span = some.shape[2]
    group = min(16, few)
    rows = count * span // STEP
    return pl.pallas_call(
        functools.partial(conv_body, tuple(pieces), sizes),
        grid=(few // group,),
        in_specs=[
            pl.BlockSpec(memory_space=pltpu.SMEM),
            *[pl.BlockSpec((some.shape[0], group, span), lambda i: (0, i, 0)) for _ in pieces],
            pl.BlockSpec((group, depth, WIDE), lambda i: (i, 0, 0)),
            pl.BlockSpec((group, LANES), lambda i: (i, 0)),
        ],
        out_specs=pl.BlockSpec((count, group, span), lambda i: (0, i, 0)),
        out_shape=jax.ShapeDtypeStruct((count, few, span), BF16),
        scratch_shapes=[
            pltpu.VMEM(((rows + WIDE // STEP) * group, LANES), F32),
            pltpu.VMEM((rows * group, LANES), F32),
        ],
        compiler_params=pltpu.CompilerParams(vmem_limit_bytes=60 << 20),
        cost_estimate=pl.CostEstimate(
            flops=2 * few * rows * depth * WIDE, bytes_accessed=few * depth * WIDE * 2, transcendentals=0
        ),
        name="long_conv",
    )(place, *pieces.values(), blocks, jnp.broadcast_to(bias[:, None], (few, LANES)))


def after(x, *others):
    return lax.optimization_barrier((x, *others))[0]


def short_conv(values, taps):
    return taps[0:1] * values + taps[1:2] * pltpu.roll(values, 1, 0) + taps[2:3] * pltpu.roll(values, 2, 0)


def project_body(token_cuts, halo_cuts, weight_cuts, out_keys, gate, counts, place, *refs):
    token_refs, weight_refs = refs[: counts[0]], refs[counts[0] : counts[0] + counts[1]]
    taps_ref, *refs = refs[counts[0] + counts[1] :]
    o_refs, (tok, tail, full, made, edge, staged, sems) = refs[: len(out_keys)], refs[len(out_keys) :]
    fr, fc, cr, cc, ch = (place[i] for i in range(5))
    blocks, rows, _ = tok.shape
    fc_n, streams = tail.shape[0], full.shape[0]
    cc_n = blocks // fc_n
    depth = weight_refs[0].shape[3]
    cr_n = 1 + max(a for _, a, _ in weight_cuts)
    feats = token_refs[0].shape[1]

    for (d, a, b), (i, j) in weight_cuts.items():
        for e in range(fc_n):
            at = ((((fr ^ d) * fc_n + (fc ^ e)) * cr_n + (cr ^ a)) * cc_n + (cc ^ b)) * depth
            cut = pl.ds(pl.multiple_of(at, depth), depth)
            pltpu.make_async_copy(weight_refs[i].at[j, e], full.at[:, cut, :], sems.at[blocks]).start()
    for (d, b), (i, start, count) in halo_cuts.items():
        cut = pl.ds(pl.multiple_of((ch ^ b) * feats, feats), feats)
        source = token_refs[i].at[pl.ds(start, count), :]
        pltpu.make_async_copy(source, tail.at[fc ^ d, :, cut], sems.at[blocks + 1]).start()
    for (d, a, b, h), (i, start, count) in token_cuts.items():
        block = (fc ^ d) * cc_n + (cc ^ a)
        cut = pl.ds(pl.multiple_of((ch ^ b) * feats, feats), feats)
        source = token_refs[i].at[pl.ds(start, count), :]
        pltpu.make_async_copy(source, tok.at[block, pl.ds(h * count, count), cut], sems.at[block]).start()
    pltpu.make_async_copy(full, full, sems.at[blocks]).wait()
    pltpu.make_async_copy(tail, tail, sems.at[blocks + 1]).wait()
    for s in range(streams):
        both = jnp.dot(tail[...].reshape(fc_n * HALO, -1), full[s], preferred_element_type=F32)
        edge[s] = both.astype(BF16).astype(F32).reshape(edge.shape[1:])

    def one_block(i, carry):
        block = (fc * cc_n + cc) ^ i
        pltpu.make_async_copy(tok.at[block], tok.at[block], sems.at[block]).wait()

        def one_stream(s, carry):
            part = jnp.dot(tok[block], full[s], preferred_element_type=F32)
            made[s, block] = part.astype(BF16).astype(F32)
            return carry

        return lax.fori_loop(0, streams, one_stream, carry)

    lax.fori_loop(0, blocks, one_block, 0)
    for block in range(blocks):
        f, c = divmod(block, cc_n)
        whole = []
        for s in range(streams):
            head = edge[s, f] if c == 0 else made[s, block - 1, rows - HALO :, :]
            whole.append(jnp.concatenate([head, made[s, block]], axis=0))
        if gate:
            one, two = (short_conv(x, taps_ref[s])[HALO:] for s, x in enumerate(whole))
            gated = (one * two).T.astype(BF16)
            few = staged.shape[2]
            for i in range(staged.shape[0]):
                staged[i, block] = gated[i * few : (i + 1) * few]
        else:
            staged[block] = whole[0].astype(BF16)
    ours, inner = (fr, cr) if gate else (fc, cc)
    copies = []
    for n, (d, a) in enumerate(out_keys):
        at = (ours ^ d) * (cr_n if gate else cc_n) + (inner ^ a)
        copies.append(pltpu.make_async_copy(staged.at[at], o_refs[n], sems.at[blocks + 2 + n]))
        copies[-1].start()
    for copy in copies:
        copy.wait()


def project(place, tokens, weights, taps, others, gate):
    arrays, token_cuts, halo_cuts = tokens
    weight_arrays, weight_cuts = weights
    _, fc_n, streams, depth, own = weight_arrays[0].shape
    rows = token_cuts[0, 0, 0, 0][2]
    blocks = fc_n * (1 + max(a for _, a, _, _ in token_cuts))
    features = arrays[0].shape[1] * (1 + max(b for _, b in halo_cuts))
    out_keys = tuple((d, a) for d in range(others[0]) for a in range(others[1]))
    few = own // len(out_keys)
    out = (blocks, few, rows) if gate else (rows + HALO, own)
    anywhere = pl.BlockSpec(memory_space=pl.ANY)
    operands = [*arrays, *weight_arrays]
    counts = (len(arrays), len(weight_arrays))
    made = pl.pallas_call(
        functools.partial(project_body, token_cuts, halo_cuts, weight_cuts, out_keys, gate, counts),
        in_specs=[
            pl.BlockSpec(memory_space=pltpu.SMEM),
            *[anywhere] * len(operands),
            pl.BlockSpec(memory_space=pltpu.VMEM),
        ],
        out_specs=[anywhere] * len(out_keys),
        out_shape=[jax.ShapeDtypeStruct(out, BF16)] * len(out_keys),
        scratch_shapes=[
            pltpu.VMEM((blocks, rows, features), BF16),
            pltpu.VMEM((fc_n, HALO, features), BF16),
            pltpu.VMEM((streams, features, own), BF16),
            pltpu.VMEM((streams, blocks, rows, own), F32),
            pltpu.VMEM((streams, fc_n, HALO, own), F32),
            pltpu.VMEM((len(out_keys), *out), BF16),
            pltpu.SemaphoreType.DMA((blocks + 2 + len(out_keys),)),
        ],
        compiler_params=pltpu.CompilerParams(vmem_limit_bytes=60 << 20),
        cost_estimate=pl.CostEstimate(
            flops=2 * blocks * rows * features * own * streams,
            bytes_accessed=2 * features * (blocks * rows + own * streams),
            transcendentals=0,
        ),
        name="project",
    )(place, *operands, taps)
    return dict(zip(out_keys, made))


def exchange(pieces, axes):
    second = lax.axis_size(axes[1])
    return {(d, a): x if (d, a) == (0, 0) else swap(x, axes, d * second + a) for (d, a), x in pieces.items()}


def combine_body(keys, sizes, place, *refs):
    fr_n, fc_n, cr_n, cc_n = sizes
    mixed_ref, taps_ref, o_ref, query, turned = refs[len(keys) :]
    own, few = turned.shape[0], mixed_ref.shape[1]
    for (d, a), ref in zip(keys, refs):
        query[(place[1] ^ d) * cc_n + (place[3] ^ a)] = ref[...].astype(F32)
    for f in range(fc_n):
        for c in range(cc_n):
            j = f * cc_n + c
            for x in range(fr_n):
                for z in range(cr_n):
                    at = (x * cr_n + z) * few
                    turned[at : at + few, :] = mixed_ref[((x * fc_n + f) * cr_n + z) * cc_n + c].astype(F32)
            cut = slice(j * own, (j + 1) * own)
            filtered = short_conv(query[j], taps_ref[:, cut])[HALO:]
            o_ref[:, cut] = (filtered * turned[...].T).astype(BF16)


def combine(place, query, mixed, taps, sizes):
    vmem = pl.BlockSpec(memory_space=pltpu.VMEM)
    rows, own = next(iter(query.values())).shape
    span = mixed.shape[2]
    groups = sizes[1] * sizes[3]
    return pl.pallas_call(
        functools.partial(combine_body, tuple(query), sizes),
        in_specs=[pl.BlockSpec(memory_space=pltpu.SMEM)] + [vmem] * (len(query) + 2),
        out_specs=vmem,
        out_shape=jax.ShapeDtypeStruct((span, groups * own), BF16),
        scratch_shapes=[pltpu.VMEM((groups, rows, own), F32), pltpu.VMEM((own, span), F32)],
        compiler_params=pltpu.CompilerParams(vmem_limit_bytes=60 << 20),
        name="combine",
    )(place, *query.values(), mixed, taps)


def tied(arrays, ties):
    return list(lax.optimization_barrier((*arrays, *ties))[: len(arrays)])


def weight_halves(streams, cut):
    fc_n, cc_n = lax.axis_size("fc"), lax.axis_size("cc")
    fc, cc = lax.axis_index("fc"), lax.axis_index("cc")
    wide = streams[0].shape[1] // fc_n
    own = wide // cc_n
    parts = []
    for e in range(fc_n):
        part = jnp.stack([lax.dynamic_slice_in_dim(w, (fc ^ e) * wide, wide, 1) for w in streams])
        parts.append(part if e == 0 else swap(part, "fc", e))

    def half(b, some):
        return jnp.stack([lax.dynamic_slice_in_dim(p[some], (cc ^ b) * own, own, 2) for p in parts])[None]

    return [[half(b, some) for b in range(cc_n)] for some in (slice(None, cut), slice(cut, None))]


def on_device(tokens, w_query, w_key, w_value, short_taps, long_filter, filter_bias):
    fr_n, fc_n, cr_n, cc_n = (lax.axis_size(a) for a in ROWS)
    fr, fc, cr, cc = (lax.axis_index(a) for a in ROWS)
    ch_n, ch = lax.axis_size("ch"), lax.axis_index("ch")
    rows = tokens.shape[0]
    part = rows // 2
    channels = w_query.shape[1]
    count = fr_n * fc_n * cr_n * cc_n
    total = count * rows
    own = channels // (cc_n * fc_n)
    few = own // (fr_n * cr_n)
    sizes = (fr_n, fc_n, cr_n, cc_n)
    place = jnp.stack([fr, fc, cr, cc, ch]).astype(jnp.int32)
    ctx = ("cr", "cc")
    first, second = [2, 1], list(range(3, cr_n * cc_n))

    def along_y(x):
        return [swap(x, "ch", b) for b in range(1, ch_n)]

    def along_x(x):
        return [swap(x, "fr", d) for d in range(1, fr_n)]

    kv, q = weight_halves([w_key, w_value, w_query], 2)
    halo = lax.ppermute(tokens[-HALO:], ROWS, [(i, i + 1) for i in range(count - 1)])
    cc_low = swap(tokens[:part], "cc", 1)
    y_own = along_y(tokens)
    kv_first = [swap(kv[k % cc_n], ctx, k) for k in first]
    kv_x0 = along_x(kv[0])
    lags = after(long_filter, *kv_x0).astype(BF16).T.reshape(fc_n, cc_n, fr_n, cr_n, few, rows)
    lags = lags.transpose(2, 0, 3, 1, 4, 5).reshape(count, few, rows)
    lags = lax.all_to_all(lags, ROWS, split_axis=0, concat_axis=0, tiled=True)
    ties = [halo, cc_low, *y_own, *kv_first, *kv_x0, lags]

    high, low, mine, kv_low, kv_high, near, lags = tied(
        [
            jnp.concatenate([tokens[part:], halo]),
            cc_low,
            jnp.concatenate([tokens, *y_own]),
            kv[0],
            kv[1],
            jnp.concatenate(kv_first),
            lags,
        ],
        ties,
    )
    kv_second = [swap((kv_low, kv_high)[k % cc_n], ctx, k) for k in second]
    kv_x1 = along_x(near)
    cc_high = swap(high, "cc", 1)
    y_low = along_y(low)
    core_own = swap(mine, "fc", 1)
    blocks = toeplitz(lags.transpose(1, 0, 2).reshape(few, total // LANES, LANES))
    ties = [*kv_second, *kv_x1, cc_high, *y_low, core_own, blocks]

    edge = jnp.where(cc == 0, halo, cc_high[part:])
    high, core_low, far, *q = tied(
        [
            jnp.concatenate([cc_high[:part], edge]),
            jnp.concatenate([cc_low, *y_low, cc_high[:part], edge]),
            jnp.concatenate(kv_second),
            *q,
        ],
        ties,
    )
    kv_x2 = along_x(far)
    y_high = along_y(high)
    core_low = swap(core_low, "fc", 1)
    q_first = [swap(q[k % cc_n], ctx, k) for k in first]
    core_high = swap(tied([jnp.concatenate(y_high)], [*kv_x2, *q_first, core_low])[0], "fc", 1)
    ties = [*kv_x2, *y_high, core_low, *q_first, core_high]

    arrays = [tokens, *y_own, core_own, cc_low, *y_low, high, *y_high, core_low, core_high]
    token_cuts, halo_cuts = {}, {}
    at = {id(x): i for i, x in enumerate(arrays)}
    for b in range(ch_n):
        source = tokens if b == 0 else y_own[b - 1]
        token_cuts[0, 0, b, 0] = (at[id(source)], 0, rows)
        token_cuts[1, 0, b, 0] = (at[id(core_own)], b * rows, rows)
        source = cc_low if b == 0 else y_low[b - 1]
        token_cuts[0, 1, b, 0] = (at[id(source)], 0, part)
        token_cuts[1, 1, b, 0] = (at[id(core_low)], b * part, part)
        source = high if b == 0 else y_high[b - 1]
        token_cuts[0, 1, b, 1] = (at[id(source)], 0, part)
        halo_cuts[0, b] = (at[id(source)], part, HALO)
        source, start = (core_low, ch_n * part) if b == 0 else (core_high, (b - 1) * (part + HALO))
        token_cuts[1, 1, b, 1] = (at[id(source)], start, part)
        halo_cuts[1, b] = (at[id(source)], start + part, HALO)
    held = (arrays, token_cuts, halo_cuts)

    def weights_of(own_piece, firsts, seconds, xs):
        sets = [([0], [own_piece]), (first, firsts), (second, seconds)]
        operands, cuts = [], {}
        for (partners, pieces), others in zip(sets, xs):
            for i, (k, piece) in enumerate(zip(partners, pieces)):
                cuts[(0, *divmod(k, cc_n))] = (len(operands), 0)
                operands.append(piece)
            for d, other in enumerate(others, 1):
                for i, k in enumerate(partners):
                    cuts[(d, *divmod(k, cc_n))] = (len(operands), i)
                operands.append(other)
        return operands, cuts

    group = (fc * cc_n + cc) * own
    taps = lax.dynamic_slice_in_dim(short_taps, group, own, 2)
    weights = weights_of(kv[0], kv_first, kv_second, (kv_x0, kv_x1, kv_x2))
    gated = project(place, held, weights, taps[1:], (fr_n, cr_n), True)
    near, *q = tied([jnp.concatenate(q_first), *q], ties)
    q_second = [swap(q[k % cc_n], ctx, k) for k in second]
    q_x0 = along_x(near)
    ties = [*q_second, *q_x0]
    keys = list(gated)
    *pieces, far = tied([*gated.values(), jnp.concatenate([q[0], *q_second])], ties)
    gated = exchange(dict(zip(keys, pieces)), ("fr", "cr"))
    q_x1 = along_x(after(far, *gated.values()))

    bias = lax.dynamic_slice_in_dim(filter_bias, group + (fr * cr_n + cr) * few, few, 0)
    mixed = long_conv(place, gated, blocks, bias, sizes)
    place, mixed = tied([place, mixed], q_x1)
    mixed = lax.all_to_all(mixed, ROWS, split_axis=0, concat_axis=0, tiled=True)

    pieces = [*q_first, q[0], *q_second]
    operands, cuts = [*pieces, *q_x0, *q_x1], {}
    for i, k in enumerate([*first, 0, *second]):
        cuts[(0, *divmod(k, cc_n))] = (i, 0)
        for d in range(1, fr_n):
            late = i >= len(first)
            at = len(pieces) + d - 1 + (fr_n - 1 if late else 0)
            cuts[(d, *divmod(k, cc_n))] = (at, i - len(first) if late else i)
    query = project(place, held, (operands, cuts), taps[:1], (fc_n, cc_n), False)
    query = exchange(query, ("fc", "cc"))
    return combine(place, query, mixed, short_taps[0], sizes)


def solution(mesh):
    f, x, h = (mesh.shape[a] for a in ("fsdp", "ctx", "ch"))
    fine = Mesh(mesh.devices.reshape(f // 2, 2, x // 2, 2, h), ROWS + ("ch",))
    spec = P(ROWS, "ch")
    return jax.shard_map(
        on_device,
        mesh=fine,
        in_specs=(spec, spec, spec, spec, P(None, None, "ch"), spec, P("ch")),
        out_specs=spec,
        check_vma=False,
    )
```
